128 devices in a mesh: dom: 16 (over x, z_hi, core), sub: 8 (over z_lo, y).
Axes of the slice: x: 4, y: 4, z: 4 (z_hi: 2, z_lo: 2; z = z_hi * 2 + z_lo), core: 2. Of those that a mesh axis runs over, the one named last changes fastest.
Arguments:
- features: float32 [262144, 128], P(('dom', 'sub')), may hold values from -6 to 6
- send_rows: int32 [128, 128, 8], P(('dom', 'sub')), may hold values from 0 to 2047
- hub_rows: int32 [128, 32], P(('dom', 'sub')), may hold values from 0 to 2047
- tile_weights: float32 [2048, 16, 128, 128], P(('dom', 'sub'))
- tile_cols: int32 [2048, 16], P(('dom', 'sub')), may hold values from 0 to 55, as said below
- tile_count: int32 [2048], P(('dom', 'sub')), may hold values from 1 to 16, as said below
- in_degree: int32 [262144], P(('dom', 'sub')), may hold values from 0 to 2048, as said below
- w_self: float32 [128, 128], replicated, may hold values from -0.5 to 0.5
- w_neigh: float32 [128, 128], replicated, may hold values from -0.5 to 0.5
- bias: float32 [128], replicated, may hold values from -3 to 3
Outputs:
- output: float32 [262144, 128], P(('dom', 'sub'))
The draws below stay inside these ranges and needn't reach their ends.
Inputs may be any that keep to these rules, and one draw needn't show every extreme that they name: `send_rows`: row indices into the sending device's own 2048 rows. `hub_rows`: row indices into the owning device's own 2048 rows. `tile_cols`: indices of 128-row blocks of the receiving device's sources. `tile_count`: some row tile holds 16 used slots in every draw; counts differ widely between devices. `in_degree`: the number of nonzero weights in the node's row over the used slots of its row tile; some node reaches 2048 in every draw.
All inputs are finite; a program needn't handle non-finite values.
Results may differ from the reference program's by a relative error of at most 0.0003.
Values sent between devices are 32-bit elements; how exact they have to be, the bound alone decides.
A program may use at most 128 MiB of HBM per device.

```python
import jax
import jax.numpy as jnp
from jax import lax

H = 128
BLK = 128
NODE_DEV = 2048
TMAX = 16
SLOT = 8
HUB_SLOT = 32
RT = 16
NODES = 262144
N_DOM = 16
N_SUB = 8
DEVICES = 128


def tile_layout(key):
    devices = NODE_DEV * 0 + DEVICES
    row_tiles = devices * (NODE_DEV // BLK)
    keys = jax.random.split(key, 9)
    heavy = jax.random.randint(keys[0], (devices,), 0, 8) == 0
    chosen = jax.random.randint(keys[1], (), 0, devices)
    heavy = jnp.logical_or(heavy, jnp.arange(devices) == chosen)
    light_top = max(1, TMAX // 4)
    dense_low = max(1, TMAX // 2)
    light_counts = jax.random.randint(keys[2], (devices, NODE_DEV // BLK), 1, light_top + 1)
    dense_counts = jax.random.randint(keys[3], (devices, NODE_DEV // BLK), dense_low, TMAX + 1)
    counts = jnp.where(heavy[:, None], dense_counts, light_counts)
    counts = counts.at[:, 0].set(jnp.where(heavy, TMAX, light_top))
    counts = counts.reshape(row_tiles).astype(jnp.int32)
    local_tiles = NODE_DEV // BLK
    halo_tiles = devices * SLOT // BLK
    hub_tiles = devices * HUB_SLOT // BLK
    category = jax.random.randint(keys[4], (row_tiles, TMAX), 0, 3)
    pick_local = jax.random.randint(keys[5], (row_tiles, TMAX), 0, local_tiles)
    pick_halo = local_tiles + jax.random.randint(keys[6], (row_tiles, TMAX), 0, halo_tiles)
    pick_hub = local_tiles + halo_tiles + jax.random.randint(keys[7], (row_tiles, TMAX), 0, hub_tiles)
    columns = jnp.where(category == 0, pick_local, jnp.where(category == 1, pick_halo, pick_hub)).astype(jnp.int32)
    edge_keys = jax.random.split(keys[8], 2)
    edges = jax.random.randint(edge_keys[0], (row_tiles, TMAX, BLK, BLK), 0, 4) == 0
    row_alive = jax.random.randint(edge_keys[1], (row_tiles, BLK), 0, 16) != 0
    edges = jnp.logical_and(edges, row_alive[:, None, :, None])
    full_tile = chosen * local_tiles
    edges = edges.at[full_tile, :, 0, :].set(True)
    slot_live = jnp.arange(TMAX)[None, :] < counts[:, None]
    live_edges = jnp.logical_and(edges, slot_live[:, :, None, None]).astype(jnp.int32)
    degree = jnp.sum(live_edges, axis=(1, 3)).reshape(row_tiles * BLK).astype(jnp.int32)
    return (counts, columns, edges, degree)


def draw_tile_weights(key, part):
    counts, columns, edges, degree = tile_layout(key)
    key = jax.random.fold_in(key, 11)
    value_key = jax.random.fold_in(key, 0)
    values = jax.random.uniform(value_key, edges.shape, jnp.float32, 0.5, 1.5)
    return jnp.where(edges, values, 0.0).astype(jnp.float32)


def draw_tile_cols(key, part):
    counts, columns, edges, degree = tile_layout(key)
    return columns


def draw_tile_count(key, part):
    counts, columns, edges, degree = tile_layout(key)
    return counts


def draw_in_degree(key, part):
    counts, columns, edges, degree = tile_layout(key)
    return degree


def with_ends(result, stream_key, smallest, largest):
    index_at = [jax.random.randint(jax.random.fold_in(stream_key, axis), (), 0, length) for axis, length in enumerate(result.shape)]
    main_axis = result.shape.index(max(result.shape))
    next_to = index_at[:main_axis] + [(index_at[main_axis] + 1) % result.shape[main_axis]] + index_at[main_axis + 1:]
    return result.at[tuple(index_at)].set(smallest).at[tuple(next_to)].set(largest)


def block_levels(stream_key, extent, cuts, least, largest):
    def one(position, parts):
        steps = jax.random.uniform(jax.random.fold_in(jax.random.fold_in(stream_key, 6), position), (parts,), jnp.float32, least / len(cuts), largest / len(cuts))
        return jnp.repeat(jnp.exp(steps), extent[position] // parts).reshape((-1,) + (1,) * (len(extent) - position - 1))

    factor_of = one(*cuts[0])
    for cut in cuts[1:]:
        factor_of = factor_of * one(*cut)
    return factor_of


def centred(own_key, dims, spread, bound, shards=(), held_as=jnp.bfloat16):
    drawn = jax.random.normal(own_key, dims, jnp.float32) * spread
    if len(shards) > 0:
        drawn = block_levels(own_key, dims, shards, -0.22, 0.18) * drawn
    return jnp.clip(drawn, min=-bound, max=bound).astype(held_as)


def setup_inputs(seed: int = 0) -> dict:
    seeds = jax.random.split(jax.random.key(seed), 11)
    return {
        "features": centred(seeds[0], (NODES, H), 1.0, 6.0, ((0, 128),), jnp.float32),
        "send_rows": with_ends(jax.random.randint(seeds[1], (DEVICES, DEVICES, SLOT), 0, NODE_DEV), jax.random.fold_in(seeds[1], 1), 0, NODE_DEV - 1).astype(jnp.int32),
        "hub_rows": with_ends(jax.random.randint(seeds[2], (DEVICES, HUB_SLOT), 0, NODE_DEV), jax.random.fold_in(seeds[2], 1), 0, NODE_DEV - 1).astype(jnp.int32),
        "tile_weights": draw_tile_weights(jax.random.fold_in(seeds[10], 71), 0),
        "tile_cols": draw_tile_cols(jax.random.fold_in(seeds[10], 71), 0),
        "tile_count": draw_tile_count(jax.random.fold_in(seeds[10], 71), 0),
        "in_degree": draw_in_degree(jax.random.fold_in(seeds[10], 71), 0),
        "w_self": centred(seeds[7], (H, H), H ** -0.5, 0.5, (), jnp.float32),
        "w_neigh": centred(seeds[8], (H, H), H ** -0.5, 0.5, (), jnp.float32),
        "bias": centred(seeds[9], (H,), 0.5, 3.0, (), jnp.float32),
    }


def reference(features, send_rows, hub_rows, tile_weights, tile_cols, tile_count, in_degree, w_self, w_neigh, bias):
    devices = N_DOM * N_SUB
    per_device = features.reshape(devices, NODE_DEV, H)
    pick_rows = jax.vmap(lambda rows_of, index_rows: rows_of[index_rows])
    hub_table = pick_rows(per_device, hub_rows).reshape(devices * HUB_SLOT, H)
    sent_rows = pick_rows(per_device, send_rows)
    by_receiver = jnp.transpose(sent_rows, (1, 0, 2, 3))
    weights_dev = tile_weights.reshape(devices, RT, TMAX, BLK, BLK)
    columns_dev = tile_cols.reshape(devices, RT, TMAX)
    counts_dev = tile_count.reshape(devices, RT)

    def one_device(packed):
        own_rows, boundary, weights, columns, counts = packed
        sources = jnp.concatenate([own_rows, boundary.reshape(devices * SLOT, H), hub_table], axis=0)
        sources = sources.reshape(-1, BLK, H)
        blocks = sources[columns]
        slot_live = (jnp.arange(TMAX)[None, :] < counts[:, None]).astype(jnp.float32)
        summed_tiles = jnp.einsum('rtij,rtjh,rt->rih', weights, blocks, slot_live, precision=lax.Precision.HIGHEST)
        return summed_tiles.reshape(NODE_DEV, H)
    summed = lax.map(one_device, (per_device, by_receiver, weights_dev, columns_dev, counts_dev)).reshape(devices * NODE_DEV, H)
    degree = jnp.maximum(in_degree, 1).astype(jnp.float32)
    neighbour_mean = summed / degree[:, None]
    hidden = jnp.dot(features, w_self, precision=lax.Precision.HIGHEST) + jnp.dot(neighbour_mean, w_neigh, precision=lax.Precision.HIGHEST) + bias
    hidden = jax.nn.relu(hidden)
    return hidden * lax.rsqrt(lax.optimization_barrier(jnp.mean(hidden * hidden, axis=-1, keepdims=True)) + 1e-05)
```

```python
import functools

import jax
import jax.numpy as jnp
from jax import lax
from jax.experimental import pallas as pl
from jax.experimental.pallas import tpu as pltpu
from jax.sharding import PartitionSpec as P

MESH = pl.DeviceIdType.MESH
H = 128
NODE = 2048
ROW_TILES = 16
SLOTS = 16
DEVICES = 128
HUB = 32
BND = 8
HUB_AT = NODE + DEVICES * BND
SOURCES = HUB_AT + DEVICES * HUB


def steps(n):
    return 0 if n == 0 else (2 if n == 2 else 1)


def hub_tree():
    nodes = [(a, b, c) for a in range(4) for b in range(4) for c in range(4)]
    levels = [[n for n in nodes if sum(v != 0 for v in n) == k] for k in range(4)]
    load = {(d, s): 0.0 for d in range(3) for s in (1, 3)}
    parent = {}
    for level in levels[1:]:
        level.sort(key=lambda n: (sum(steps(v) for v in n), n))
        for n in level:
            best = None
            for d in range(3):
                if n[d] == 0:
                    continue
                uses = [(d, 1), (d, 3)] if n[d] == 2 else [(d, n[d])]
                key = (steps(n[d]), max(load[u] for u in uses), d)
                if best is None or key < best[0]:
                    best = (key, d, uses)
            _, d, uses = best
            for u in uses:
                load[u] += 1.0
            parent[n] = tuple(0 if i == d else v for i, v in enumerate(n))
    order = [n for level in levels for n in level]
    return levels, order, parent


LEVELS, ORDER, PARENT = hub_tree()
SLOT_OF = {n: i for i, n in enumerate(ORDER)}
CHILDREN = {n: [m for m in ORDER if PARENT.get(m) == n] for n in ORDER}
SWAPS = [(0, 1), (1, 9), (10, 27), (37, 27)]


def coords():
    dom = lax.axis_index("dom")
    sub = lax.axis_index("sub")
    z = lax.rem(lax.div(dom, 2), 2) * 2 + lax.div(sub, 4)
    return lax.div(dom, 4), lax.rem(sub, 4), z, lax.rem(dom, 2)


def device_at(x, y, z, c):
    return x * 4 + lax.div(z, 2) * 2 + c, lax.rem(z, 2) * 4 + y


def far_first(k):
    def offset(high, low):
        return jnp.where(high == 0, 2 - low, 3 * (1 - low))

    c = lax.rem(k, 2)
    h = lax.div(k, 16)
    low = lax.rem(lax.div(k, 2), 8)
    x = offset(lax.div(h, 4), lax.div(low, 4))
    y = offset(lax.rem(lax.div(h, 2), 2), lax.rem(lax.div(low, 2), 2))
    z = offset(lax.rem(h, 2), lax.rem(low, 2))
    return x, y, z, 1 - c


def split(v):
    hi = v.astype(jnp.bfloat16)
    lo = (v - hi.astype(jnp.float32)).astype(jnp.bfloat16)
    return hi, lo


def kernel(
    features,
    send_rows,
    hub_rows,
    weights,
    cols,
    count,
    degree,
    w_self,
    w_neigh,
    bias,
    out,
    feat,
    stage,
    parts,
    src,
    bnd_out,
    bnd,
    hub,
    hub_other,
    mean,
    base,
    feat_sem,
    stage_sem,
    hub_send,
    hub_recv,
    swap_send,
    swap_recv,
    bnd_send,
    bnd_recv,
):
    X, Y, Z, C = coords()

    def partner(x, y, z, c):
        return device_at(
            lax.rem(X + x, 4), lax.rem(Y + y, 4), lax.rem(Z + z, 4), lax.rem(C + c, 2)
        )

    barrier = pltpu.get_barrier_semaphore()

    def greet(k, _):
        pl.semaphore_signal(
            barrier, 1, device_id=partner(*far_first(k)), device_id_type=MESH
        )
        return 0

    lax.fori_loop(0, DEVICES - 1, greet, 0)

    feat_copy = pltpu.make_async_copy(features, feat, feat_sem)
    feat_copy.start()
    stage_copies = []
    for r in range(ROW_TILES):
        copy = pltpu.make_async_copy(weights.at[r], stage.at[r], stage_sem.at[r])
        copy.start()
        stage_copies.append(copy)

    feat_copy.wait()
    for i in range(HUB):
        hub[0, i] = feat[hub_rows[0, i]]
    pl.semaphore_wait(barrier, DEVICES - 1)

    def hub_copy(n):
        p = PARENT[n]
        move = tuple((a - b) % 4 for a, b in zip(n, p))
        return pltpu.make_async_remote_copy(
            src_ref=hub.at[SLOT_OF[p]],
            dst_ref=hub.at[SLOT_OF[n]],
            send_sem=hub_send,
            recv_sem=hub_recv.at[SLOT_OF[n]],
            device_id=partner(*move, 0),
            device_id_type=MESH,
        )

    def swap_copy(i):
        first, size = SWAPS[i]
        return pltpu.make_async_remote_copy(
            src_ref=hub.at[pl.ds(first, size)],
            dst_ref=hub_other.at[pl.ds(first, size)],
            send_sem=swap_send,
            recv_sem=swap_recv.at[i],
            device_id=partner(0, 0, 0, 1),
            device_id_type=MESH,
        )

    for n in CHILDREN[(0, 0, 0)]:
        hub_copy(n).start()
    swap_copy(0).start()

    me_dom = lax.axis_index("dom")
    me_sub = lax.axis_index("sub")
    me = me_dom * 8 + me_sub

    def gather(p, dst):
        for j in range(BND):
            dst[p, j] = feat[send_rows[j, p]]

    def send_boundary(k, _):
        dom, sub = partner(*far_first(k))
        p = dom * 8 + sub
        gather(p, bnd_out)
        pltpu.make_async_remote_copy(
            src_ref=bnd_out.at[p],
            dst_ref=bnd.at[me],
            send_sem=bnd_send,
            recv_sem=bnd_recv,
            device_id=(dom, sub),
            device_id_type=MESH,
        ).start()
        return 0

    lax.fori_loop(0, DEVICES - 1, send_boundary, 0)
    gather(me, bnd)

    def put(block, at, rows):
        hi, lo = split(rows)
        src[block, pl.ds(at, rows.shape[0]), 0:H] = hi
        src[block, pl.ds(at, rows.shape[0]), H:] = lo

    def put_features(i, _):
        at = pl.multiple_of(i * 128, 128)
        put(i, 0, feat[pl.ds(at, 128), :])
        return 0

    def convert(r):
        stage_copies[r].wait()
        deg = jnp.maximum(degree[r : r + 1, :], 1).astype(jnp.float32)
        scale = jnp.transpose(jnp.broadcast_to(1.0 / deg, (H, H)))

        def one(t, _):
            live = jnp.clip(count[r] - t, 0, 1).astype(jnp.float32)
            hi, lo = split(stage[r, t] * (scale * live))
            parts[r, t, 0:H, :] = hi
            parts[r, t, H:, :] = lo
            return 0

        lax.fori_loop(0, SLOTS, one, 0)

    def put_hub(table, core, level):
        for n in level:
            x, y, z = (lax.rem(v + 4 - o, 4) for v, o in zip((X, Y, Z), n))
            dom, sub = device_at(x, y, z, core)
            block = HUB_AT // 128 + dom * 2 + lax.div(sub, 4)
            at = pl.multiple_of(lax.rem(sub, 4) * HUB, HUB)
            put(block, at, table[SLOT_OF[n]])

    def arrive(level):
        for n in LEVELS[level]:
            hub_copy(n).wait_recv()
            for m in CHILDREN[n]:
                hub_copy(m).start()
        swap_copy(level).start()

    lax.fori_loop(0, ROW_TILES, put_features, 0)
    for r in range(0, 4):
        convert(r)
    arrive(1)
    put_hub(hub, C, LEVELS[0])
    put_hub(hub, C, LEVELS[1])
    for r in range(4, 8):
        convert(r)
    arrive(2)
    put_hub(hub, C, LEVELS[2])
    for r in range(8, 12):
        convert(r)
    ws_hi, ws_lo = split(w_self[...])
    both = jnp.concatenate([ws_hi, ws_hi], axis=0)

    def self_term(i, _):
        at = pl.multiple_of(i * 128, 128)
        rows = src[i]
        total = jnp.dot(rows, both, preferred_element_type=jnp.float32)
        total += jnp.dot(rows[:, 0:H], ws_lo, preferred_element_type=jnp.float32)
        base[pl.ds(at, 128), :] = total + bias[...]
        return 0

    lax.fori_loop(0, ROW_TILES, self_term, 0)
    for r in range(12, 16):
        convert(r)
    arrive(3)
    put_hub(hub, C, LEVELS[3])
    for i in range(4):
        swap_copy(i).wait_recv()
        put_hub(hub_other, 1 - C, LEVELS[i])
    others = pl.ds(0, DEVICES - 1)
    pltpu.make_async_copy(bnd_out.at[others], bnd.at[others], bnd_recv).wait()

    def put_boundary(i, _):
        rows = bnd[pl.ds(i * 16, 16)].reshape(128, H)
        put(NODE // 128 + i, 0, rows)
        return 0

    lax.fori_loop(0, DEVICES // 16, put_boundary, 0)

    def row_tile(r, _):
        lhs = jnp.concatenate([parts[r, t] for t in range(SLOTS)], axis=1)
        rhs = jnp.concatenate(
            [src[cols[r, t]] for t in range(SLOTS)], axis=0
        )
        res = jnp.dot(lhs, rhs, preferred_element_type=jnp.float32)
        total = (res[0:H, 0:H] + res[H:, H:]) + (res[0:H, H:] + res[H:, 0:H])
        mean[pl.ds(pl.multiple_of(r * 128, 128), 128), :] = total
        return 0

    lax.fori_loop(0, ROW_TILES, row_tile, 0)

    wn_hi, wn_lo = split(w_neigh[...])
    three = jnp.concatenate([wn_hi, wn_hi, wn_lo], axis=0)

    def finish(i, _):
        at = pl.multiple_of(i * 256, 256)
        hi, lo = split(mean[pl.ds(at, 256), :])
        rows = jnp.concatenate([hi, lo, hi], axis=1)
        hidden = base[pl.ds(at, 256), :] + jnp.dot(
            rows, three, preferred_element_type=jnp.float32
        )
        hidden = jnp.maximum(hidden, 0.0)
        square = jnp.mean(hidden * hidden, axis=-1, keepdims=True)
        out[pl.ds(at, 256), :] = hidden * lax.rsqrt(square + 1e-05)
        return 0

    lax.fori_loop(0, NODE // 256, finish, 0)

    tree = pl.ds(0, len(ORDER) - 1)
    pltpu.make_async_copy(hub.at[tree], hub.at[tree], hub_send).wait()
    pltpu.make_async_copy(hub, hub_other, swap_send).wait()
    pltpu.make_async_copy(bnd_out.at[others], bnd.at[others], bnd_send).wait()


def body(
    features,
    send_rows,
    hub_rows,
    tile_weights,
    tile_cols,
    tile_count,
    in_degree,
    w_self,
    w_neigh,
    bias,
):
    f32, bf16 = jnp.float32, jnp.bfloat16
    any_ = pl.BlockSpec(memory_space=pl.ANY)
    smem = pl.BlockSpec(memory_space=pltpu.SMEM)
    vmem = pl.BlockSpec(memory_space=pltpu.VMEM)
    dma = pltpu.SemaphoreType.DMA
    return pl.pallas_call(
        kernel,
        out_shape=jax.ShapeDtypeStruct((NODE, H), f32),
        in_specs=[any_, smem, smem, any_, smem, smem, vmem, vmem, vmem, vmem],
        out_specs=vmem,
        scratch_shapes=[
            pltpu.VMEM((NODE, H), f32),
            pltpu.VMEM((ROW_TILES, SLOTS, H, H), f32),
            pltpu.VMEM((ROW_TILES, SLOTS, 2 * H, H), bf16),
            pltpu.VMEM((SOURCES // 128, 128, 2 * H), bf16),
            pltpu.VMEM((DEVICES, BND, H), f32),
            pltpu.VMEM((DEVICES, BND, H), f32),
            pltpu.VMEM((64, HUB, H), f32),
            pltpu.VMEM((64, HUB, H), f32),
            pltpu.VMEM((NODE, H), f32),
            pltpu.VMEM((NODE, H), f32),
            dma,
            dma((ROW_TILES,)),
            dma,
            dma((64,)),
            dma,
            dma((4,)),
            dma,
            dma,
        ],
        compiler_params=pltpu.CompilerParams(
            collective_id=0, has_side_effects=True, vmem_limit_bytes=56 << 20
        ),
    )(
        features,
        jnp.swapaxes(send_rows, 1, 2).reshape(BND, DEVICES),
        hub_rows,
        tile_weights,
        tile_cols,
        tile_count,
        in_degree.reshape(ROW_TILES, H),
        w_self,
        w_neigh,
        bias.reshape(1, H),
    )


def solution(mesh):
    in_specs = (
        P(("dom", "sub"), None),
        P(("dom", "sub"), None, None),
        P(("dom", "sub"), None),
        P(("dom", "sub"), None, None, None),
        P(("dom", "sub"), None),
        P(("dom", "sub")),
        P(("dom", "sub")),
        P(),
        P(),
        P(),
    )
    out_specs = P(("dom", "sub"), None)
    return jax.shard_map(body, mesh=mesh, in_specs=in_specs, out_specs=out_specs, check_vma=False)
```

```python
import jax
import jax.numpy as jnp
from jax import lax
from jax.experimental import pallas as pl
from jax.experimental.pallas import tpu as pltpu
from jax.sharding import PartitionSpec as P

MESH = pl.DeviceIdType.MESH
H = 128
NODE = 2048
ROW_TILES = 16
SLOTS = 16
DEVICES = 128
HUB = 32
BND = 8
LOCAL_BLOCKS = NODE // 128
BND_BLOCKS = DEVICES * BND // 128
HUB_BLOCK = LOCAL_BLOCKS + BND_BLOCKS
BLOCKS = HUB_BLOCK + DEVICES * HUB // 128


def steps(n):
    return 0 if n == 0 else (2 if n == 2 else 1)


def distance(n):
    return sum(steps(v) for v in n)


def hub_tree():
    nodes = [(a, b, c) for a in range(4) for b in range(4) for c in range(4)]
    levels = [[n for n in nodes if sum(v != 0 for v in n) == k] for k in range(4)]
    load = {(d, s): 0.0 for d in range(3) for s in (1, 3)}
    parent = {}
    for level in levels[1:]:
        level.sort(key=lambda n: (distance(n), n))
        for n in level:
            best = None
            for d in range(3):
                if n[d] == 0:
                    continue
                uses = [(d, 1), (d, 3)] if n[d] == 2 else [(d, n[d])]
                key = (steps(n[d]), max(load[u] for u in uses), d)
                if best is None or key < best[0]:
                    best = (key, d, uses)
            _, d, uses = best
            for u in uses:
                load[u] += 1.0
            parent[n] = tuple(0 if i == d else v for i, v in enumerate(n))
    order = [n for level in levels for n in level]
    return levels, order, parent


LEVELS, ORDER, PARENT = hub_tree()
SLOT_OF = {n: i for i, n in enumerate(ORDER)}
CHILDREN = {n: [m for m in ORDER if PARENT.get(m) == n] for n in ORDER}
SWAPS = [(0, 1), (1, 9)] + [(10 + 9 * i, 9) for i in range(6)]
FAR_FIRST = sorted(
    ((x, y, z, c) for x in range(4) for y in range(4) for z in range(4) for c in range(2)),
    key=lambda n: (-distance(n[:3]), n),
)[:-2] + [(0, 0, 0, 1)]


def split(v):
    hi = v.astype(jnp.bfloat16)
    lo = (v - hi.astype(jnp.float32)).astype(jnp.bfloat16)
    return hi, lo


def kernel(
    features,
    send_rows_in,
    hub_rows_in,
    weights,
    cols_in,
    count_in,
    degree_in,
    w_self_in,
    w_neigh_in,
    bias_in,
    out,
    feat,
    send_rows,
    hub_rows,
    cols,
    count,
    degree,
    w_self,
    w_neigh,
    bias,
    stage,
    parts,
    src,
    bnd_out,
    bnd,
    hub,
    hub_other,
    base,
    small_sem,
    stage_sem,
    hub_send,
    hub_recv,
    swap_send,
    swap_recv,
    bnd_send,
    bnd_recv,
):
    dom = lax.axis_index("dom")
    sub = lax.axis_index("sub")
    me = dom * 8 + sub

    def partner(x, y, z, c=0):
        return dom ^ (x * 4 + (z // 2) * 2 + c), sub ^ ((z % 2) * 4 + y)

    barrier = pltpu.get_barrier_semaphore()
    for n in FAR_FIRST:
        pl.semaphore_signal(barrier, 1, device_id=partner(*n), device_id_type=MESH)

    fetched = []
    for i, (a, b) in enumerate(
        [
            (hub_rows_in, hub_rows),
            (features, feat),
            (send_rows_in, send_rows),
            (count_in, count),
            (degree_in, degree),
            (w_self_in, w_self),
            (w_neigh_in, w_neigh),
            (bias_in, bias),
            (cols_in, cols),
        ]
    ):
        copy = pltpu.make_async_copy(a, b, small_sem.at[i])
        copy.start()
        fetched.append(copy)
    stage_copies = []
    for r in range(ROW_TILES):
        copy = pltpu.make_async_copy(weights.at[r], stage.at[r], stage_sem.at[r])
        copy.start()
        stage_copies.append(copy)

    fetched[0].wait()
    fetched[1].wait()
    for i in range(HUB):
        hub[0, i] = feat[hub_rows[0, i]]
    pl.semaphore_wait(barrier, DEVICES - 1)

    def hub_copy(n):
        p = PARENT[n]
        return pltpu.make_async_remote_copy(
            src_ref=hub.at[SLOT_OF[p]],
            dst_ref=hub.at[SLOT_OF[n]],
            send_sem=hub_send,
            recv_sem=hub_recv.at[SLOT_OF[n]],
            device_id=partner(*(a ^ b for a, b in zip(n, p))),
            device_id_type=MESH,
        )

    def swap_copy(i):
        first, size = SWAPS[i]
        return pltpu.make_async_remote_copy(
            src_ref=hub.at[pl.ds(first, size)],
            dst_ref=hub_other.at[pl.ds(first, size)],
            send_sem=swap_send,
            recv_sem=swap_recv.at[i],
            device_id=partner(0, 0, 0, 1),
            device_id_type=MESH,
        )

    for n in CHILDREN[(0, 0, 0)]:
        hub_copy(n).start()
    swap_copy(0).start()

    fetched[2].wait()
    for n in FAR_FIRST:
        to = partner(*n)
        p = to[0] * 8 + to[1]
        for j in range(BND):
            bnd_out[p, j] = feat[send_rows[j, p]]
        pltpu.make_async_remote_copy(
            src_ref=bnd_out.at[p],
            dst_ref=bnd.at[me],
            send_sem=bnd_send,
            recv_sem=bnd_recv,
            device_id=to,
            device_id_type=MESH,
        ).start()
    for j in range(BND):
        bnd[me, j] = feat[send_rows[j, me]]

    def put(block, at, rows):
        hi, lo = split(rows)
        src[block, pl.ds(at, rows.shape[0]), 0:H] = hi
        src[block, pl.ds(at, rows.shape[0]), H:] = lo

    def put_features(i, _):
        put(i, 0, feat[pl.ds(pl.multiple_of(i * 128, 128), 128), :])
        return 0

    def convert(r):
        stage_copies[r].wait()
        deg = jnp.maximum(degree[r : r + 1, :], 1).astype(jnp.float32)
        scale = jnp.transpose(jnp.broadcast_to(1.0 / deg, (H, H)))

        def one(t, _):
            live = jnp.clip(count[r] - t, 0, 1).astype(jnp.float32)
            hi, lo = split(stage[r, t] * (scale * live))
            parts[r, t, 0:H, :] = hi
            parts[r, t, H:, :] = lo
            return 0

        lax.fori_loop(0, SLOTS, one, 0, unroll=4)

    def put_hub(table, core, nodes):
        for n in nodes:
            d, s = partner(*n)
            d = (d // 2) * 2 + core
            block = HUB_BLOCK + d * 2 + s // 4
            at = pl.multiple_of((s % 4) * HUB, HUB)
            put(block, at, table[SLOT_OF[n]])

    def arrive(level):
        for n in LEVELS[level]:
            hub_copy(n).wait_recv()
            for m in CHILDREN[n]:
                hub_copy(m).start()
            for i, (first, size) in enumerate(SWAPS):
                if SLOT_OF[n] == first + size - 1:
                    swap_copy(i).start()

    core = dom % 2
    fetched[3].wait()
    fetched[4].wait()
    for r in range(0, 3):
        convert(r)
    arrive(1)
    put_hub(hub, core, LEVELS[0] + LEVELS[1])
    for r in range(3, 8):
        convert(r)
    arrive(2)
    put_hub(hub, core, LEVELS[2])
    for r in range(8, 12):
        convert(r)
    lax.fori_loop(0, LOCAL_BLOCKS, put_features, 0)
    for copy in fetched[5:]:
        copy.wait()
    ws_hi, ws_lo = split(w_self[...])
    both = jnp.concatenate([ws_hi, ws_hi], axis=0)

    def self_term(i, _):
        rows = src[i]
        total = jnp.dot(rows, both, preferred_element_type=jnp.float32)
        total += jnp.dot(rows[:, 0:H], ws_lo, preferred_element_type=jnp.float32)
        base[pl.ds(pl.multiple_of(i * 128, 128), 128), :] = total + bias[...]
        return 0

    lax.fori_loop(0, ROW_TILES, self_term, 0, unroll=4)
    for r in range(12, 16):
        convert(r)
    arrive(3)
    put_hub(hub, core, LEVELS[3])
    for i, (first, size) in enumerate(SWAPS):
        swap_copy(i).wait_recv()
        put_hub(hub_other, 1 - core, ORDER[first : first + size])
    others = pl.ds(0, DEVICES - 1)
    pltpu.make_async_copy(bnd_out.at[others], bnd.at[others], bnd_recv).wait()

    def put_boundary(i, _):
        put(LOCAL_BLOCKS + i, 0, bnd[pl.ds(i * 16, 16)].reshape(128, H))
        return 0

    lax.fori_loop(0, BND_BLOCKS, put_boundary, 0)

    wn_hi, wn_lo = split(w_neigh[...])
    three = jnp.concatenate([wn_hi, wn_hi, wn_lo], axis=0)

    def row_tile(r):
        lhs = jnp.concatenate([parts[r, t] for t in range(SLOTS)], axis=1)
        rhs = jnp.concatenate([src[cols[r, t]] for t in range(SLOTS)], axis=0)
        res = jnp.dot(lhs, rhs, preferred_element_type=jnp.float32)
        return (res[0:H, 0:H] + res[H:, H:]) + (res[0:H, H:] + res[H:, 0:H])

    group = 4
    for g in range(0, ROW_TILES, group):
        rows = pl.ds(g * 128, group * 128)
        mean = jnp.concatenate([row_tile(g + i) for i in range(group)], axis=0)
        hi, lo = split(mean)
        hidden = base[rows, :] + jnp.dot(
            jnp.concatenate([hi, lo, hi], axis=1),
            three,
            preferred_element_type=jnp.float32,
        )
        hidden = jnp.maximum(hidden, 0.0)
        square = jnp.mean(hidden * hidden, axis=-1, keepdims=True)
        out[rows, :] = hidden * lax.rsqrt(square + 1e-05)

    tree = pl.ds(0, len(ORDER) - 1)
    pltpu.make_async_copy(hub.at[tree], hub.at[tree], hub_send).wait()
    pltpu.make_async_copy(hub, hub_other, swap_send).wait()
    pltpu.make_async_copy(bnd_out.at[others], bnd.at[others], bnd_send).wait()


def body(
    features,
    send_rows,
    hub_rows,
    tile_weights,
    tile_cols,
    tile_count,
    in_degree,
    w_self,
    w_neigh,
    bias,
):
    f32, bf16, i32 = jnp.float32, jnp.bfloat16, jnp.int32
    dma = pltpu.SemaphoreType.DMA
    vmem, smem = pltpu.VMEM, pltpu.SMEM
    return pl.pallas_call(
        kernel,
        out_shape=vmem((NODE, H), f32),
        in_specs=[pl.BlockSpec(memory_space=pl.ANY)] * 10,
        out_specs=pl.BlockSpec(memory_space=vmem),
        scratch_shapes=[
            vmem((NODE, H), f32),
            smem((BND, DEVICES), i32),
            smem((1, HUB), i32),
            smem((ROW_TILES, SLOTS), i32),
            smem((ROW_TILES,), i32),
            vmem((ROW_TILES, H), i32),
            vmem((H, H), f32),
            vmem((H, H), f32),
            vmem((1, H), f32),
            vmem((ROW_TILES, SLOTS, H, H), f32),
            vmem((ROW_TILES, SLOTS, 2 * H, H), bf16),
            vmem((BLOCKS, 128, 2 * H), bf16),
            vmem((DEVICES, BND, H), f32),
            vmem((DEVICES, BND, H), f32),
            vmem((64, HUB, H), f32),
            vmem((64, HUB, H), f32),
            vmem((NODE, H), f32),
            dma((9,)),
            dma((ROW_TILES,)),
            dma,
            dma((64,)),
            dma,
            dma((len(SWAPS),)),
            dma,
            dma,
        ],
        compiler_params=pltpu.CompilerParams(
            collective_id=0, has_side_effects=True, vmem_limit_bytes=56 << 20
        ),
    )(
        features,
        jnp.swapaxes(send_rows, 1, 2).reshape(BND, DEVICES),
        hub_rows,
        tile_weights,
        tile_cols,
        tile_count,
        in_degree.reshape(ROW_TILES, H),
        w_self,
        w_neigh,
        bias.reshape(1, H),
    )


def solution(mesh):
    in_specs = (
        P(("dom", "sub"), None),
        P(("dom", "sub"), None, None),
        P(("dom", "sub"), None),
        P(("dom", "sub"), None, None, None),
        P(("dom", "sub"), None),
        P(("dom", "sub")),
        P(("dom", "sub")),
        P(),
        P(),
        P(),
    )
    out_specs = P(("dom", "sub"), None)
    return jax.shard_map(body, mesh=mesh, in_specs=in_specs, out_specs=out_specs, check_vma=False)
```

```python
import jax
import jax.numpy as jnp
from jax import lax
from jax.experimental import pallas as pl
from jax.experimental.pallas import tpu as pltpu
from jax.sharding import PartitionSpec as P

MESH = pl.DeviceIdType.MESH
H = 128
NODE = 2048
ROW_TILES = 16
SLOTS = 16
DEVICES = 128
HUB = 32
BND = 8
LOCAL_BLOCKS = NODE // 128
BND_BLOCKS = DEVICES * BND // 128
HUB_BLOCK = LOCAL_BLOCKS + BND_BLOCKS
BLOCKS = HUB_BLOCK + DEVICES * HUB // 128


def steps(n):
    return 0 if n == 0 else (2 if n == 2 else 1)


def distance(n):
    return sum(steps(v) for v in n)


def hub_tree():
    nodes = [(a, b, c) for a in range(4) for b in range(4) for c in range(4)]
    levels = [[n for n in nodes if sum(v != 0 for v in n) == k] for k in range(4)]
    load = {(d, s): 0.0 for d in range(3) for s in (1, 3)}
    parent = {}
    for level in levels[1:]:
        level.sort(key=lambda n: (distance(n), n))
        for n in level:
            best = None
            for d in range(3):
                if n[d] == 0:
                    continue
                uses = [(d, 1), (d, 3)] if n[d] == 2 else [(d, n[d])]
                key = (steps(n[d]), max(load[u] for u in uses), d)
                if best is None or key < best[0]:
                    best = (key, d, uses)
            _, d, uses = best
            for u in uses:
                load[u] += 1.0
            parent[n] = tuple(0 if i == d else v for i, v in enumerate(n))
    order = [n for level in levels for n in level]
    return levels, order, parent


LEVELS, ORDER, PARENT = hub_tree()
SLOT_OF = {n: i for i, n in enumerate(ORDER)}
CHILDREN = {n: [m for m in ORDER if PARENT.get(m) == n] for n in ORDER}
SWAPS = [(0, 1), (1, 9)] + [(10 + 9 * i, 9) for i in range(6)]
def link_uses(n):
    uses = []
    for d, v in enumerate(n[:3]):
        uses += [(d, 1)] * (v in (1, 2)) + [(d, 3)] * (v in (2, 3))
    return uses


def spread_out(nodes):
    load = {(d, s): 0.0 for d in range(3) for s in (1, 3)}
    left, result = list(nodes), []
    while left:

        def cost(n):
            uses = link_uses(n)
            return (load[uses[0]] * 3 + sum(load[u] for u in uses[1:])) / len(uses), n

        best = min(left, key=cost)
        left.remove(best)
        result.append(best)
        for u in load:
            load[u] *= 0.7
        for u in link_uses(best):
            load[u] += 1.0
    return result


def link_uses(n):
    uses = []
    for d, v in enumerate(n[:3]):
        uses += [(d, 1)] * (v in (1, 2)) + [(d, 3)] * (v in (2, 3))
    return uses


def spread_out(nodes):
    load = {(d, s): 0.0 for d in range(3) for s in (1, 3)}
    left, result = list(nodes), []
    while left:

        def cost(n):
            uses = link_uses(n)
            return (load[uses[0]] * 3 + sum(load[u] for u in uses[1:])) / len(uses), n

        best = min(left, key=cost)
        left.remove(best)
        result.append(best)
        for u in load:
            load[u] *= 0.7
        for u in link_uses(best):
            load[u] += 1.0
    return result


FAR_FIRST = sorted(
    ((x, y, z, c) for x in range(4) for y in range(4) for z in range(4) for c in range(2)),
    key=lambda n: (-distance(n[:3]), n),
)[:-2] + [(0, 0, 0, 1)]


def both_cores(nodes):
    first = [n + (i % 2,) for i, n in enumerate(nodes)]
    return first + [(x, y, z, 1 - c) for x, y, z, c in first]


EXCHANGE = [both_cores(spread_out(level)) for level in LEVELS[1:]]
EXCHANGE[0].append((0, 0, 0, 1))


def split(v):
    hi = v.astype(jnp.bfloat16)
    lo = (v - hi.astype(jnp.float32)).astype(jnp.bfloat16)
    return hi, lo


def kernel(
    features,
    send_rows_in,
    hub_rows_in,
    weights,
    cols_in,
    count_in,
    degree_in,
    w_self_in,
    w_neigh_in,
    bias_in,
    out,
    feat,
    send_rows,
    hub_rows,
    cols,
    count,
    degree,
    w_self,
    w_neigh,
    bias,
    stage,
    parts,
    src,
    bnd_out,
    bnd,
    hub,
    hub_other,
    base,
    small_sem,
    stage_sem,
    hub_send,
    hub_recv,
    swap_send,
    swap_recv,
    plane_sem,
    cube_sem,
    bnd_send,
    bnd_recv,
):
    dom = lax.axis_index("dom")
    sub = lax.axis_index("sub")
    me = dom * 8 + sub

    def partner(x, y, z, c=0):
        return dom ^ (x * 4 + (z // 2) * 2 + c), sub ^ ((z % 2) * 4 + y)

    barrier = pltpu.get_barrier_semaphore()
    for n in EXCHANGE[0]:
        pl.semaphore_signal(barrier, 1, device_id=partner(*n), device_id_type=MESH)

    fetched = []
    for i, (a, b) in enumerate(
        [
            (hub_rows_in, hub_rows),
            (features, feat),
            (send_rows_in, send_rows),
            (count_in, count),
            (degree_in, degree),
            (w_self_in, w_self),
            (w_neigh_in, w_neigh),
            (bias_in, bias),
            (cols_in, cols),
        ]
    ):
        copy = pltpu.make_async_copy(a, b, small_sem.at[i])
        copy.start()
        fetched.append(copy)
    stage_copies = []
    for r in range(ROW_TILES):
        copy = pltpu.make_async_copy(weights.at[r], stage.at[r], stage_sem.at[r])
        stage_copies.append(copy)

    fetched[0].wait()
    fetched[1].wait()
    for i in range(HUB):
        hub[0, i] = feat[hub_rows[0, i]]
    pl.semaphore_wait(barrier, len(EXCHANGE[0]))

    def tell(sem):
        for n in LEVELS[1]:
            pl.semaphore_signal(sem, 1, device_id=partner(*n), device_id_type=MESH)

    def hub_copy(n):
        p = PARENT[n]
        return pltpu.make_async_remote_copy(
            src_ref=hub.at[SLOT_OF[p]],
            dst_ref=hub.at[SLOT_OF[n]],
            send_sem=hub_send,
            recv_sem=hub_recv.at[SLOT_OF[n]],
            device_id=partner(*(a ^ b for a, b in zip(n, p))),
            device_id_type=MESH,
        )

    def swap_copy(i):
        first, size = SWAPS[i]
        return pltpu.make_async_remote_copy(
            src_ref=hub.at[pl.ds(first, size)],
            dst_ref=hub_other.at[pl.ds(first, size)],
            send_sem=swap_send,
            recv_sem=swap_recv.at[i],
            device_id=partner(0, 0, 0, 1),
            device_id_type=MESH,
        )

    for n in CHILDREN[(0, 0, 0)]:
        hub_copy(n).start()
    swap_copy(0).start()
    tell(plane_sem)

    fetched[2].wait()
    def send_boundary(nodes):
      for n in nodes:
        to = partner(*n)
        p = to[0] * 8 + to[1]
        for j in range(BND):
            bnd_out[p, j] = feat[send_rows[j, p]]
        pltpu.make_async_remote_copy(
            src_ref=bnd_out.at[p],
            dst_ref=bnd.at[me],
            send_sem=bnd_send,
            recv_sem=bnd_recv,
            device_id=to,
            device_id_type=MESH,
        ).start()
    send_boundary(EXCHANGE[0])
    for c in stage_copies: c.start()
    for j in range(BND):
        bnd[me, j] = feat[send_rows[j, me]]

    def put(block, at, rows):
        hi, lo = split(rows)
        src[block, pl.ds(at, rows.shape[0]), 0:H] = hi
        src[block, pl.ds(at, rows.shape[0]), H:] = lo

    def put_features(i, _):
        put(i, 0, feat[pl.ds(pl.multiple_of(i * 128, 128), 128), :])
        return 0

    def convert(r):
        stage_copies[r].wait()
        deg = jnp.maximum(degree[r : r + 1, :], 1).astype(jnp.float32)
        scale = jnp.transpose(jnp.broadcast_to(1.0 / deg, (H, H)))

        def one(t, _):
            live = jnp.clip(count[r] - t, 0, 1).astype(jnp.float32)
            hi, lo = split(stage[r, t] * (scale * live))
            parts[r, t, 0:H, :] = hi
            parts[r, t, H:, :] = lo
            return 0

        lax.fori_loop(0, SLOTS, one, 0, unroll=4)

    def put_hub(table, core, nodes):
        for n in nodes:
            d, s = partner(*n)
            d = (d // 2) * 2 + core
            block = HUB_BLOCK + d * 2 + s // 4
            at = pl.multiple_of((s % 4) * HUB, HUB)
            put(block, at, table[SLOT_OF[n]])

    def arrive(level):
        for n in LEVELS[level]:
            hub_copy(n).wait_recv()
            for m in CHILDREN[n]:
                hub_copy(m).start()
            for i, (first, size) in enumerate(SWAPS):
                if SLOT_OF[n] == first + size - 1:
                    swap_copy(i).start()

    core = dom % 2
    fetched[3].wait()
    fetched[4].wait()
    pl.semaphore_wait(plane_sem, len(LEVELS[1]))
    tell(cube_sem)
    send_boundary(EXCHANGE[1])
    for r in range(0, 3):
        convert(r)
    arrive(1)
    pl.semaphore_wait(cube_sem, len(LEVELS[1]))
    send_boundary(EXCHANGE[2][:27])
    put_hub(hub, core, LEVELS[0] + LEVELS[1])
    for r in range(3, 8):
        convert(r)
    arrive(2)
    send_boundary(EXCHANGE[2][27:])
    put_hub(hub, core, LEVELS[2])
    for r in range(8, 12):
        convert(r)
    lax.fori_loop(0, LOCAL_BLOCKS, put_features, 0)
    for copy in fetched[5:]:
        copy.wait()
    ws_hi, ws_lo = split(w_self[...])
    both = jnp.concatenate([ws_hi, ws_hi], axis=0)

    def self_term(i, _):
        rows = src[i]
        total = jnp.dot(rows, both, preferred_element_type=jnp.float32)
        total += jnp.dot(rows[:, 0:H], ws_lo, preferred_element_type=jnp.float32)
        base[pl.ds(pl.multiple_of(i * 128, 128), 128), :] = total + bias[...]
        return 0

    lax.fori_loop(0, ROW_TILES, self_term, 0, unroll=4)
    for r in range(12, 16):
        convert(r)
    arrive(3)
    put_hub(hub, core, LEVELS[3])
    for i, (first, size) in enumerate(SWAPS):
        swap_copy(i).wait_recv()
        put_hub(hub_other, 1 - core, ORDER[first : first + size])
    others = pl.ds(0, DEVICES - 1)
    pltpu.make_async_copy(bnd_out.at[others], bnd.at[others], bnd_recv).wait()

    def put_boundary(i, _):
        put(LOCAL_BLOCKS + i, 0, bnd[pl.ds(i * 16, 16)].reshape(128, H))
        return 0

    lax.fori_loop(0, BND_BLOCKS, put_boundary, 0)

    wn_hi, wn_lo = split(w_neigh[...])
    three = jnp.concatenate([wn_hi, wn_hi, wn_lo], axis=0)

    def row_tile(r):
        lhs = jnp.concatenate([parts[r, t] for t in range(SLOTS)], axis=1)
        rhs = jnp.concatenate([src[cols[r, t]] for t in range(SLOTS)], axis=0)
        res = jnp.dot(lhs, rhs, preferred_element_type=jnp.float32)
        return (res[0:H, 0:H] + res[H:, H:]) + (res[0:H, H:] + res[H:, 0:H])

    group = 4
    for g in range(0, ROW_TILES, group):
        rows = pl.ds(g * 128, group * 128)
        mean = jnp.concatenate([row_tile(g + i) for i in range(group)], axis=0)
        hi, lo = split(mean)
        hidden = base[rows, :] + jnp.dot(
            jnp.concatenate([hi, lo, hi], axis=1),
            three,
            preferred_element_type=jnp.float32,
        )
        hidden = jnp.maximum(hidden, 0.0)
        square = jnp.mean(hidden * hidden, axis=-1, keepdims=True)
        out[rows, :] = hidden * lax.rsqrt(square + 1e-05)

    tree = pl.ds(0, len(ORDER) - 1)
    pltpu.make_async_copy(hub.at[tree], hub.at[tree], hub_send).wait()
    pltpu.make_async_copy(hub, hub_other, swap_send).wait()
    pltpu.make_async_copy(bnd_out.at[others], bnd.at[others], bnd_send).wait()


def body(
    features,
    send_rows,
    hub_rows,
    tile_weights,
    tile_cols,
    tile_count,
    in_degree,
    w_self,
    w_neigh,
    bias,
):
    f32, bf16, i32 = jnp.float32, jnp.bfloat16, jnp.int32
    dma = pltpu.SemaphoreType.DMA
    vmem, smem = pltpu.VMEM, pltpu.SMEM
    return pl.pallas_call(
        kernel,
        out_shape=vmem((NODE, H), f32),
        in_specs=[pl.BlockSpec(memory_space=pl.ANY)] * 10,
        out_specs=pl.BlockSpec(memory_space=vmem),
        scratch_shapes=[
            vmem((NODE, H), f32),
            smem((BND, DEVICES), i32),
            smem((1, HUB), i32),
            smem((ROW_TILES, SLOTS), i32),
            smem((ROW_TILES,), i32),
            vmem((ROW_TILES, H), i32),
            vmem((H, H), f32),
            vmem((H, H), f32),
            vmem((1, H), f32),
            vmem((ROW_TILES, SLOTS, H, H), f32),
            vmem((ROW_TILES, SLOTS, 2 * H, H), bf16),
            vmem((BLOCKS, 128, 2 * H), bf16),
            vmem((DEVICES, BND, H), f32),
            vmem((DEVICES, BND, H), f32),
            vmem((64, HUB, H), f32),
            vmem((64, HUB, H), f32),
            vmem((NODE, H), f32),
            dma((9,)),
            dma((ROW_TILES,)),
            dma,
            dma((64,)),
            dma,
            dma((len(SWAPS),)),
            pltpu.SemaphoreType.REGULAR,
            pltpu.SemaphoreType.REGULAR,
            dma,
            dma,
        ],
        compiler_params=pltpu.CompilerParams(
            collective_id=0, has_side_effects=True, vmem_limit_bytes=56 << 20
        ),
    )(
        features,
        jnp.swapaxes(send_rows, 1, 2).reshape(BND, DEVICES),
        hub_rows,
        tile_weights,
        tile_cols,
        tile_count,
        in_degree.reshape(ROW_TILES, H),
        w_self,
        w_neigh,
        bias.reshape(1, H),
    )


def solution(mesh):
    in_specs = (
        P(("dom", "sub"), None),
        P(("dom", "sub"), None, None),
        P(("dom", "sub"), None),
        P(("dom", "sub"), None, None, None),
        P(("dom", "sub"), None),
        P(("dom", "sub")),
        P(("dom", "sub")),
        P(),
        P(),
        P(),
    )
    out_specs = P(("dom", "sub"), None)
    return jax.shard_map(body, mesh=mesh, in_specs=in_specs, out_specs=out_specs, check_vma=False)
```

```python
import jax
import jax.numpy as jnp
from jax import lax
from jax.experimental import pallas as pl
from jax.experimental.pallas import tpu as pltpu
from jax.sharding import PartitionSpec as P

MESH = pl.DeviceIdType.MESH
H = 128
NODE = 2048
ROW_TILES = 16
SLOTS = 16
DEVICES = 128
HUB = 32
BND = 8
LOCAL_BLOCKS = NODE // 128
BND_BLOCKS = DEVICES * BND // 128
HUB_BLOCK = LOCAL_BLOCKS + BND_BLOCKS
BLOCKS = HUB_BLOCK + DEVICES * HUB // 128


def steps(n):
    return 0 if n == 0 else (2 if n == 2 else 1)


def distance(n):
    return sum(steps(v) for v in n)


def hub_tree():
    nodes = [(a, b, c) for a in range(4) for b in range(4) for c in range(4)]
    levels = [[n for n in nodes if sum(v != 0 for v in n) == k] for k in range(4)]
    load = {(d, s): 0.0 for d in range(3) for s in (1, 3)}
    parent = {}
    for level in levels[1:]:
        level.sort(key=lambda n: (distance(n), n))
        for n in level:
            best = None
            for d in range(3):
                if n[d] == 0:
                    continue
                uses = [(d, 1), (d, 3)] if n[d] == 2 else [(d, n[d])]
                key = (steps(n[d]), max(load[u] for u in uses), d)
                if best is None or key < best[0]:
                    best = (key, d, uses)
            _, d, uses = best
            for u in uses:
                load[u] += 1.0
            parent[n] = tuple(0 if i == d else v for i, v in enumerate(n))
    order = [n for level in levels for n in level]
    return levels, order, parent


LEVELS, ORDER, PARENT = hub_tree()
SLOT_OF = {n: i for i, n in enumerate(ORDER)}
CHILDREN = {n: [m for m in ORDER if PARENT.get(m) == n] for n in ORDER}
SWAPS = [(0, 1), (1, 9)] + [(10 + 9 * i, 9) for i in range(6)]
def link_uses(n):
    uses = []
    for d, v in enumerate(n[:3]):
        uses += [(d, 1)] * (v in (1, 2)) + [(d, 3)] * (v in (2, 3))
    return uses


def spread_out(nodes):
    load = {(d, s): 0.0 for d in range(3) for s in (1, 3)}
    left, result = list(nodes), []
    while left:

        def cost(n):
            uses = link_uses(n)
            return (load[uses[0]] * 3 + sum(load[u] for u in uses[1:])) / len(uses), n

        best = min(left, key=cost)
        left.remove(best)
        result.append(best)
        for u in load:
            load[u] *= 0.7
        for u in link_uses(best):
            load[u] += 1.0
    return result


def link_uses(n):
    uses = []
    for d, v in enumerate(n[:3]):
        uses += [(d, 1)] * (v in (1, 2)) + [(d, 3)] * (v in (2, 3))
    return uses


def spread_out(nodes):
    load = {(d, s): 0.0 for d in range(3) for s in (1, 3)}
    left, result = list(nodes), []
    while left:

        def cost(n):
            uses = link_uses(n)
            return (load[uses[0]] * 3 + sum(load[u] for u in uses[1:])) / len(uses), n

        best = min(left, key=cost)
        left.remove(best)
        result.append(best)
        for u in load:
            load[u] *= 0.7
        for u in link_uses(best):
            load[u] += 1.0
    return result


FAR_FIRST = sorted(
    ((x, y, z, c) for x in range(4) for y in range(4) for z in range(4) for c in range(2)),
    key=lambda n: (-distance(n[:3]), n),
)[:-2] + [(0, 0, 0, 1)]


def both_cores(nodes):
    first = [n + (i % 2,) for i, n in enumerate(nodes)]
    return first + [(x, y, z, 1 - c) for x, y, z, c in first]


EXCHANGE = [both_cores(spread_out(level)) for level in LEVELS[1:]]
EXCHANGE[0].append((0, 0, 0, 1))


def split(v):
    hi = v.astype(jnp.bfloat16)
    lo = (v - hi.astype(jnp.float32)).astype(jnp.bfloat16)
    return hi, lo


def kernel(
    features,
    send_rows_in,
    hub_rows_in,
    weights,
    cols_in,
    count_in,
    degree_in,
    w_self_in,
    w_neigh_in,
    bias_in,
    out,
    feat,
    send_rows,
    hub_rows,
    cols,
    count,
    degree,
    w_self,
    w_neigh,
    bias,
    stage,
    parts,
    src,
    bnd_out,
    bnd,
    hub,
    hub_other,
    base,
    small_sem,
    stage_sem,
    hub_send,
    hub_recv,
    swap_send,
    swap_recv,
    plane_sem,
    cube_sem,
    bnd_send,
    bnd_recv,
):
    dom = lax.axis_index("dom")
    sub = lax.axis_index("sub")
    me = dom * 8 + sub

    def partner(x, y, z, c=0):
        return dom ^ (x * 4 + (z // 2) * 2 + c), sub ^ ((z % 2) * 4 + y)

    barrier = pltpu.get_barrier_semaphore()
    for n in EXCHANGE[0]:
        pl.semaphore_signal(barrier, 1, device_id=partner(*n), device_id_type=MESH)

    fetched = []
    for i, (a, b) in enumerate(
        [
            (hub_rows_in, hub_rows),
            (features, feat),
            (send_rows_in, send_rows),
            (count_in, count),
            (degree_in, degree),
            (w_self_in, w_self),
            (w_neigh_in, w_neigh),
            (bias_in, bias),
            (cols_in, cols),
        ]
    ):
        copy = pltpu.make_async_copy(a, b, small_sem.at[i])
        copy.start()
        fetched.append(copy)
    stage_copies = []
    for r in range(ROW_TILES):
        copy = pltpu.make_async_copy(weights.at[r], stage.at[r], stage_sem.at[r])
        stage_copies.append(copy)

    pl.semaphore_wait(barrier, len(EXCHANGE[0]))

    def tell(sem):
        for n in LEVELS[1]:
            pl.semaphore_signal(sem, 1, device_id=partner(*n), device_id_type=MESH)

    def hub_copy(n):
        p = PARENT[n]
        return pltpu.make_async_remote_copy(
            src_ref=hub.at[SLOT_OF[p]],
            dst_ref=hub.at[SLOT_OF[n]],
            send_sem=hub_send,
            recv_sem=hub_recv.at[SLOT_OF[n]],
            device_id=partner(*(a ^ b for a, b in zip(n, p))),
            device_id_type=MESH,
        )

    def swap_copy(i):
        first, size = SWAPS[i]
        return pltpu.make_async_remote_copy(
            src_ref=hub.at[pl.ds(first, size)],
            dst_ref=hub_other.at[pl.ds(first, size)],
            send_sem=swap_send,
            recv_sem=swap_recv.at[i],
            device_id=partner(0, 0, 0, 1),
            device_id_type=MESH,
        )

    tell(plane_sem)
    fetched[0].wait()
    fetched[1].wait()
    for i in range(HUB):
        hub[0, i] = feat[hub_rows[0, i]]
    for n in CHILDREN[(0, 0, 0)]:
        hub_copy(n).start()
    swap_copy(0).start()

    fetched[2].wait()
    def send_boundary(nodes):
      for n in nodes:
        to = partner(*n)
        p = to[0] * 8 + to[1]
        for j in range(BND):
            bnd_out[p, j] = feat[send_rows[j, p]]
        pltpu.make_async_remote_copy(
            src_ref=bnd_out.at[p],
            dst_ref=bnd.at[me],
            send_sem=bnd_send,
            recv_sem=bnd_recv,
            device_id=to,
            device_id_type=MESH,
        ).start()
    send_boundary(EXCHANGE[0])
    for c in stage_copies: c.start()
    for j in range(BND):
        bnd[me, j] = feat[send_rows[j, me]]

    def put(block, at, rows):
        hi, lo = split(rows)
        src[block, pl.ds(at, rows.shape[0]), 0:H] = hi
        src[block, pl.ds(at, rows.shape[0]), H:] = lo

    def put_features(i, _):
        put(i, 0, feat[pl.ds(pl.multiple_of(i * 128, 128), 128), :])
        return 0

    def convert(r):
        stage_copies[r].wait()
        deg = jnp.maximum(degree[r : r + 1, :], 1).astype(jnp.float32)
        scale = jnp.transpose(jnp.broadcast_to(1.0 / deg, (H, H)))

        def one(t, _):
            live = jnp.clip(count[r] - t, 0, 1).astype(jnp.float32)
            hi, lo = split(stage[r, t] * (scale * live))
            parts[r, t, 0:H, :] = hi
            parts[r, t, H:, :] = lo
            return 0

        lax.fori_loop(0, SLOTS, one, 0, unroll=4)

    def put_hub(table, core, nodes):
        for n in nodes:
            d, s = partner(*n)
            d = (d // 2) * 2 + core
            block = HUB_BLOCK + d * 2 + s // 4
            at = pl.multiple_of((s % 4) * HUB, HUB)
            put(block, at, table[SLOT_OF[n]])

    def arrive(level):
        for n in LEVELS[level]:
            hub_copy(n).wait_recv()
            for m in CHILDREN[n]:
                hub_copy(m).start()
            for i, (first, size) in enumerate(SWAPS):
                if SLOT_OF[n] == first + size - 1:
                    swap_copy(i).start()

    core = dom % 2
    fetched[3].wait()
    fetched[4].wait()
    pl.semaphore_wait(plane_sem, len(LEVELS[1]))
    tell(cube_sem)
    send_boundary(EXCHANGE[1])
    for r in range(0, 3):
        convert(r)
    arrive(1)
    pl.semaphore_wait(cube_sem, len(LEVELS[1]))
    send_boundary(EXCHANGE[2][:27])
    put_hub(hub, core, LEVELS[0] + LEVELS[1])
    for r in range(3, 8):
        convert(r)
    arrive(2)
    send_boundary(EXCHANGE[2][27:])
    put_hub(hub, core, LEVELS[2])
    for r in range(8, 12):
        convert(r)
    lax.fori_loop(0, LOCAL_BLOCKS, put_features, 0)
    for copy in fetched[5:]:
        copy.wait()
    ws_hi, ws_lo = split(w_self[...])
    both = jnp.concatenate([ws_hi, ws_hi], axis=0)

    wn_hi, wn_lo = split(w_neigh[...])
    three = jnp.concatenate([wn_hi, wn_hi, wn_lo], axis=0)

    def self_term(i, _):
        rows = src[i]
        total = jnp.dot(rows, both, preferred_element_type=jnp.float32)
        total += jnp.dot(rows[:, 0:H], ws_lo, preferred_element_type=jnp.float32)
        base[pl.ds(pl.multiple_of(i * 128, 128), 128), :] = total + bias[...]
        return 0

    lax.fori_loop(0, ROW_TILES, self_term, 0, unroll=4)
    for r in range(12, 16):
        convert(r)
    arrive(3)
    put_hub(hub, core, LEVELS[3])
    for i, (first, size) in enumerate(SWAPS):
        swap_copy(i).wait_recv()
        put_hub(hub_other, 1 - core, ORDER[first : first + size])
    others = pl.ds(0, DEVICES - 1)
    pltpu.make_async_copy(bnd_out.at[others], bnd.at[others], bnd_recv).wait()

    def put_boundary(i, _):
        put(LOCAL_BLOCKS + i, 0, bnd[pl.ds(i * 16, 16)].reshape(128, H))
        return 0

    lax.fori_loop(0, BND_BLOCKS, put_boundary, 0, unroll=True)

    def row_tile(r):
        lhs = jnp.concatenate([parts[r, t] for t in range(SLOTS)], axis=1)
        rhs = jnp.concatenate([src[cols[r, t]] for t in range(SLOTS)], axis=0)
        res = jnp.dot(lhs, rhs, preferred_element_type=jnp.float32)
        return (res[0:H, 0:H] + res[H:, H:]) + (res[0:H, H:] + res[H:, 0:H])

    group = 8
    for g in range(0, ROW_TILES, group):
        rows = pl.ds(g * 128, group * 128)
        mean = jnp.concatenate([row_tile(g + i) for i in range(group)], axis=0)
        hi, lo = split(mean)
        hidden = base[rows, :] + jnp.dot(
            jnp.concatenate([hi, lo, hi], axis=1),
            three,
            preferred_element_type=jnp.float32,
        )
        hidden = jnp.maximum(hidden, 0.0)
        square = jnp.mean(hidden * hidden, axis=-1, keepdims=True)
        out[rows, :] = hidden * lax.rsqrt(square + 1e-05)

    tree = pl.ds(0, len(ORDER) - 1)
    pltpu.make_async_copy(hub.at[tree], hub.at[tree], hub_send).wait()
    pltpu.make_async_copy(hub, hub_other, swap_send).wait()
    pltpu.make_async_copy(bnd_out.at[others], bnd.at[others], bnd_send).wait()


def body(
    features,
    send_rows,
    hub_rows,
    tile_weights,
    tile_cols,
    tile_count,
    in_degree,
    w_self,
    w_neigh,
    bias,
):
    f32, bf16, i32 = jnp.float32, jnp.bfloat16, jnp.int32
    dma = pltpu.SemaphoreType.DMA
    vmem, smem = pltpu.VMEM, pltpu.SMEM
    return pl.pallas_call(
        kernel,
        out_shape=vmem((NODE, H), f32),
        in_specs=[pl.BlockSpec(memory_space=pl.ANY)] * 10,
        out_specs=pl.BlockSpec(memory_space=vmem),
        scratch_shapes=[
            vmem((NODE, H), f32),
            smem((BND, DEVICES), i32),
            smem((1, HUB), i32),
            smem((ROW_TILES, SLOTS), i32),
            smem((ROW_TILES,), i32),
            vmem((ROW_TILES, H), i32),
            vmem((H, H), f32),
            vmem((H, H), f32),
            vmem((1, H), f32),
            vmem((ROW_TILES, SLOTS, H, H), f32),
            vmem((ROW_TILES, SLOTS, 2 * H, H), bf16),
            vmem((BLOCKS, 128, 2 * H), bf16),
            vmem((DEVICES, BND, H), f32),
            vmem((DEVICES, BND, H), f32),
            vmem((64, HUB, H), f32),
            vmem((64, HUB, H), f32),
            vmem((NODE, H), f32),
            dma((9,)),
            dma((ROW_TILES,)),
            dma,
            dma((64,)),
            dma,
            dma((len(SWAPS),)),
            pltpu.SemaphoreType.REGULAR,
            pltpu.SemaphoreType.REGULAR,
            dma,
            dma,
        ],
        compiler_params=pltpu.CompilerParams(
            collective_id=0, has_side_effects=True, vmem_limit_bytes=56 << 20
        ),
    )(
        features,
        jnp.swapaxes(send_rows, 1, 2).reshape(BND, DEVICES),
        hub_rows,
        tile_weights,
        tile_cols,
        tile_count,
        in_degree.reshape(ROW_TILES, H),
        w_self,
        w_neigh,
        bias.reshape(1, H),
    )


def solution(mesh):
    in_specs = (
        P(("dom", "sub"), None),
        P(("dom", "sub"), None, None),
        P(("dom", "sub"), None),
        P(("dom", "sub"), None, None, None),
        P(("dom", "sub"), None),
        P(("dom", "sub")),
        P(("dom", "sub")),
        P(),
        P(),
        P(),
    )
    out_specs = P(("dom", "sub"), None)
    return jax.shard_map(body, mesh=mesh, in_specs=in_specs, out_specs=out_specs, check_vma=False)
```
